32 devices in a mesh: lane: 8 (over z, core), rec: 4 (over y, x).
Axes of the slice: x: 2, y: 2, z: 4, core: 2. Of those that a mesh axis runs over, the one named last changes fastest.
Arguments:
- waveforms: bfloat16 [128, 16384], P('lane', 'rec'), may hold values from -6 to 6
- patterns: int32 [128, 16384], P('lane', 'rec'), may hold values from 0 to 3
- partners: int32 [128, 8], P('lane'), may hold values from 0 to 127, as said below
- counts: int32 [128], P('lane'), may hold values from 1 to 8, as said below
Outputs:
- responses: float32 [2, 256, 1024], P(None, 'rec', 'lane')
The draws below stay inside these ranges and needn't reach their ends.
Inputs may be any that keep to these rules, and one draw needn't show every extreme that they name: partners[l, s] is never l; the 8 partners of a lane lie on 8 different indices of lane; of the 128 entries of the lanes of one index of lane, exactly 16 name lanes of each index of lane. `counts`: uneven over lanes and over indices of lane.
All inputs are finite; a program needn't handle non-finite values.
Results may differ from the reference program's by a relative error of at most 0.0003.
Values may be sent and summed in bfloat16 or wider, within the bound.
A program may use at most 64 MiB of HBM per device.

```python
import jax
import jax.numpy as jnp
from jax import lax

LANE_DEV = 16
SLOTS = 8
LAGS = 256
LANES = 128
TIME = 16384
N_LANE = 8


def draw_partners(key, part):
    key_order, key_local = jax.random.split(jax.random.fold_in(key, 7))
    orders = jax.vmap(lambda single: jax.random.permutation(single, N_LANE))(jax.random.split(key_order, N_LANE))
    serial = jnp.arange(LANE_DEV * SLOTS, dtype=jnp.int32)
    target_dev = orders[:, serial % N_LANE].astype(jnp.int32)
    owner = jnp.arange(N_LANE, dtype=jnp.int32)[:, None]
    own_lane = serial[None, :] // SLOTS
    local = jax.random.randint(key_local, (N_LANE, LANE_DEV * SLOTS), 0, LANE_DEV).astype(jnp.int32)
    local = jnp.where((target_dev == owner) & (local == own_lane), (local + 1) % LANE_DEV, local)
    return (target_dev * LANE_DEV + local).reshape(LANES, SLOTS).astype(jnp.int32)


def draw_counts(key, part):
    key_hot, key_pick, key_count = jax.random.split(jax.random.fold_in(key, 13), 3)
    heavy = jax.random.randint(key_hot, (N_LANE,), 0, 8) == 0
    forced = jax.random.randint(key_pick, (), 0, N_LANE)
    heavy = heavy | (jnp.arange(N_LANE, dtype=jnp.int32) == forced)
    lane_heavy = jnp.repeat(heavy, LANE_DEV)
    light = jax.random.randint(key_count, (LANES,), 1, SLOTS // 2 + 1)
    return jnp.where(lane_heavy, SLOTS, light).astype(jnp.int32)


def set_ends(result, rng, smallest, top_value):
    place = [jax.random.randint(jax.random.fold_in(rng, axis), (), 0, length) for axis, length in enumerate(result.shape)]
    main_axis = result.shape.index(max(result.shape))
    neighbour = place[:main_axis] + [(place[main_axis] + 1) % result.shape[main_axis]] + place[main_axis + 1:]
    return result.at[tuple(place)].set(smallest).at[tuple(neighbour)].set(top_value)


def block_scale(stream_key, dims, cuts, low, top_value):
    gain = 1.0
    for position, parts in cuts:
        draws = jax.random.uniform(jax.random.fold_in(jax.random.fold_in(stream_key, 6), position), (parts,), jnp.float32, low / len(cuts), top_value / len(cuts))
        gain = gain * jnp.repeat(jnp.exp(draws), dims[position] // parts).reshape((-1,) + (1,) * (len(dims) - 1 - position))
    return gain


def noise(rng, shape, width, limit, cuts=(), kind=jnp.bfloat16):
    entries = jax.random.normal(rng, shape, jnp.float32) * width
    if len(cuts) > 0:
        entries = block_scale(rng, shape, cuts, -0.22, 0.18) * entries
    return jnp.clip(entries, min=-limit, max=limit).astype(kind)


def setup_inputs(seed: int = 0) -> dict:
    key_of = jax.random.split(jax.random.key(seed), 5)
    waveforms = noise(key_of[0], (LANES, TIME), 1.0, 6.0, ((0, 8), (1, 4)))
    patterns = set_ends(jax.random.randint(key_of[1], (LANES, TIME), 0, 4), jax.random.fold_in(key_of[1], 1), 0, 3).astype(jnp.int32)
    partners = draw_partners(jax.random.fold_in(key_of[4], 71), 0)
    counts = draw_counts(jax.random.fold_in(key_of[4], 71), 0)
    return {"waveforms": waveforms, "patterns": patterns, "partners": partners, "counts": counts}


def reference(waveforms, patterns, partners, counts):
    length = 2 * TIME
    signal = jnp.fft.rfft(waveforms.astype(jnp.float32), n=length, axis=1)
    levels = (2 * patterns - 3).astype(jnp.float32)
    spectra = jnp.fft.rfft(levels, n=length, axis=1)

    def one_lane(lane):
        chosen = partners[lane]
        forward = jnp.fft.irfft(signal[lane][None, :] * jnp.conj(spectra[chosen]), n=length, axis=1)[:, :LAGS]
        reverse = jnp.fft.irfft(signal[chosen] * jnp.conj(spectra[lane])[None, :], n=length, axis=1)[:, :LAGS]
        return forward, reverse

    forward, reverse = lax.map(one_lane, jnp.arange(LANES, dtype=jnp.int32))
    valid = (jnp.arange(SLOTS, dtype=jnp.int32)[None, :] < counts[:, None]).astype(jnp.float32)
    scale = (5.0 * TIME) ** -0.5
    both = jnp.stack([forward, reverse]) * valid[None, :, :, None] * scale
    both = jnp.transpose(both, (0, 3, 1, 2)).reshape(2, LAGS, LANES * SLOTS)
    return both.astype(jnp.float32)
```

```python
import functools

import jax
import jax.numpy as jnp
from jax import lax
from jax.experimental import pallas as pl
from jax.experimental.pallas import tpu as pltpu
from jax.sharding import PartitionSpec as P

LAGS = 256
FINE = 16
STEPS = LAGS // FINE
MESH = pl.DeviceIdType.MESH
F32 = jnp.float32
BF16 = jnp.bfloat16


def nn(a, b):
    return lax.dot_general(a, b, (((1,), (0,)), ((), ())), preferred_element_type=F32)


def nt(a, b):
    return lax.dot_general(a, b, (((1,), (1,)), ((), ())), preferred_element_type=F32)


def pieces(x, count):
    parts = []
    for _ in range(count):
        part = x.astype(BF16)
        parts.append(part)
        x = x - part.astype(F32)
    return parts


def iota(shape, axis):
    return lax.broadcasted_iota(jnp.int32, shape, axis)


def kernel(
    n_lane, n_rec, slots, scale, chunks,
    w_ref, pat_ref, meta_ref, out_ref,
    wall, metas, rim, halo, shifted, refs, acc, zbuf, zin, fout, fin,
    send_d, recv_d, send_s, recv_s, send_m, recv_m, send_h, recv_h,
    send_z, recv_z, send_f, recv_f,
):
    lane_dev, time_dev = w_ref.shape
    lanes = lane_dev * n_lane
    pairs = lane_dev * slots
    n_z = n_lane // 2
    lag_dev = LAGS // n_rec
    per_rec = STEPS // n_rec
    cols = FINE * lane_dev
    wide = time_dev // chunks
    me = lax.axis_index("lane")
    rec = lax.axis_index("rec")
    z, core = me // 2, me % 2
    sibling = 2 * z + 1 - core

    barrier = pltpu.get_barrier_semaphore()
    for off in range(1, n_lane):
        pl.semaphore_signal(
            barrier, inc=1, device_id={"lane": (me + off) % n_lane}, device_id_type=MESH
        )
    for off in range(1, n_rec):
        pl.semaphore_signal(
            barrier, inc=1, device_id={"rec": (rec + off) % n_rec}, device_id_type=MESH
        )

    def rows_of(owner):
        return pl.ds(pl.multiple_of(owner * lane_dev, lane_dev), lane_dev)

    def remote(src, dst, send, recv, where):
        return pltpu.make_async_remote_copy(
            src_ref=src, dst_ref=dst, send_sem=send, recv_sem=recv,
            device_id=where, device_id_type=MESH,
        )

    levels = (2 * pat_ref[...] - 3).astype(F32)
    rim[...] = levels[:, time_dev - LAGS :].astype(BF16)
    metas[rows_of(me), :] = meta_ref[...]
    wall[rows_of(me), :] = w_ref[...]

    pl.semaphore_wait(barrier, n_lane - 1 + n_rec - 1)

    sent = []
    to_next = remote(rim, halo, send_h.at[0], recv_h.at[0], {"rec": (rec + 1) % n_rec})
    to_next.start()
    sent.append(to_next)

    def span(c):
        return pl.ds(c * wide, wide)

    def direct(off, c):
        return remote(
            w_ref.at[:, span(c)], wall.at[rows_of(me), span(c)],
            send_d.at[off, c], recv_d.at[off, c],
            {"lane": 2 * ((z + off) % n_z) + core},
        )

    def arrived(off, c):
        block = wall.at[rows_of(2 * ((z + n_z - off) % n_z) + core), span(c)]
        return remote(block, block, send_d.at[off, c], recv_d.at[off, c], {"lane": sibling})

    def across(off, c):
        block = wall.at[rows_of(2 * ((z + n_z - off) % n_z) + core), span(c)]
        return remote(block, block, send_s.at[off, c], recv_s.at[off, c], {"lane": sibling})

    def crossed(off, c):
        block = wall.at[rows_of(2 * ((z + n_z - off) % n_z) + 1 - core), span(c)]
        return remote(block, block, send_s.at[off, c], recv_s.at[off, c], {"lane": sibling})

    for c in range(chunks):
        for off in range(1, n_z):
            copy = direct(off, c)
            copy.start()
            sent.append(copy)
        copy = across(0, c)
        copy.start()
        sent.append(copy)
    for off in range(1, n_lane):
        copy = remote(
            meta_ref, metas.at[rows_of(me), :], send_m.at[off], recv_m.at[off],
            {"lane": (me + off) % n_lane},
        )
        copy.start()
        sent.append(copy)

    to_next.wait_recv()
    before = jnp.where(rec > 0, halo[...].astype(F32), 0.0)
    extended = jnp.concatenate([before, levels], axis=1)
    for r in range(FINE):
        moved = extended if r == 0 else pltpu.roll(extended, r, 1)
        shifted[r * lane_dev : (r + 1) * lane_dev, :] = moved.astype(BF16)
    unit = (iota((LAGS, LAGS), 0) == iota((LAGS, LAGS), 1)).astype(BF16)
    for b in range((time_dev + LAGS) // LAGS):
        part = slice(b * LAGS, (b + 1) * LAGS)
        refs[part, :] = nt(unit, shifted[:, part]).astype(BF16)

    def multiply(c):
        group = 4

        def body(step, carry):
            for i in range(group):
                a = step * group + i
                start = pl.multiple_of(c * wide + LAGS - FINE * a, FINE)
                term = nn(wall[:, c * wide : (c + 1) * wide], refs[pl.ds(start, wide), :])
                if c == 0:
                    acc[a] = term
                else:
                    acc[a] += term
            return carry

        lax.fori_loop(0, STEPS // group, body, 0)

    for c in range(chunks + 1):
        if c < chunks:
            for off in range(1, n_z):
                arrived(off, c).wait_recv()
                copy = across(off, c)
                copy.start()
                sent.append(copy)
        if c > 0:
            for off in range(n_z):
                crossed(off, c - 1).wait_recv()
            multiply(c - 1)

    for off in range(1, n_lane):
        owner = (me + n_lane - off) % n_lane
        block = metas.at[rows_of(owner), :]
        remote(block, block, send_m.at[off], recv_m.at[off], {"lane": sibling}).wait_recv()
    every = metas[...]
    inside = every - me * lane_dev
    mine = (inside >= 0) & (inside < lane_dev) & (iota(every.shape, 1) < slots)
    named = jnp.sum(jnp.where(mine, (inside + 1).astype(F32), 0.0), axis=1, keepdims=True) - 1.0
    column_lane = iota((lanes, cols), 1) % lane_dev
    keep_forward = named == column_lane.astype(F32)
    own = meta_ref[...]
    spread = (iota((pairs, lane_dev), 0) // slots == iota((pairs, lane_dev), 1)).astype(BF16)
    low, high = own % 64, own // 64
    tall = 64.0 * nn(spread, high.astype(F32).astype(BF16)) + nn(spread, low.astype(F32).astype(BF16))
    at_slot = iota(tall.shape, 1) == iota(tall.shape, 0) % slots
    target = jnp.sum(jnp.where(at_slot, tall, 0.0), axis=1, keepdims=True).astype(jnp.int32)
    pick = (target == iota((pairs, lanes), 1)).astype(BF16)
    keep_reverse = iota((pairs, cols), 1) % lane_dev == iota((pairs, cols), 0) // slots
    place = (
        (target // lane_dev) * lane_dev + iota((pairs, lanes), 0) // slots
        == iota((pairs, lanes), 1)
    ).astype(BF16)
    gather = (iota((FINE, cols), 1) // lane_dev == iota((FINE, cols), 0)).astype(BF16)
    pair_row = iota((lane_dev, pairs), 1)
    listed = (pair_row // slots == iota((lane_dev, pairs), 0)) & (
        pair_row % slots < own[:, slots : slots + 1]
    )
    gain = jnp.sum(jnp.where(listed, F32(scale), 0.0), axis=0, keepdims=True)

    for off in list(range(1, n_rec)) + [0]:
        there = (rec + off) % n_rec
        for i in range(per_rec):
            full = acc[there * per_rec + i]
            total_f = jnp.zeros((FINE, lanes), F32)
            total_r = jnp.zeros((FINE, pairs), F32)
            for part in pieces(full, 2):
                forward = jnp.where(keep_forward, part.astype(F32), 0.0).astype(BF16)
                total_f += nt(gather, forward)
                reverse = jnp.where(keep_reverse, nn(pick, part), 0.0).astype(BF16)
                total_r += nt(gather, reverse)
            zbuf[off, i * FINE : (i + 1) * FINE, 0:lanes] = total_f
            zbuf[off, i * FINE : (i + 1) * FINE, lanes : lanes + pairs] = total_r
        if off > 0:
            copy = remote(
                zbuf.at[off], zin.at[off], send_z.at[off], recv_z.at[off], {"rec": there}
            )
            copy.start()
            sent.append(copy)

    total = zbuf[0]
    for off in range(1, n_rec):
        remote(
            zbuf.at[off], zin.at[off], send_z.at[off], recv_z.at[off], {"lane": sibling}
        ).wait_recv()
        total += zin[off]

    line = (iota((lanes, lanes), 0) == iota((lanes, lanes), 1)).astype(BF16)
    forward_sum = total[:, 0:lanes]
    if lag_dev < 128:
        forward_sum = jnp.concatenate(
            [forward_sum, jnp.zeros((128 - lag_dev, lanes), F32)], axis=0
        )
    turned = jnp.zeros((lanes, 128), F32)
    for part in pieces(forward_sum, 3):
        turned += nt(line, part)
    fout[...] = turned
    fin[rows_of(me), :] = fout[rows_of(me), :]
    for off in range(1, n_lane):
        there = (me + off) % n_lane
        copy = remote(
            fout.at[rows_of(there), :], fin.at[rows_of(me), :],
            send_f.at[off], recv_f.at[off], {"lane": there},
        )
        copy.start()
        sent.append(copy)
    out_ref[1] = total[:, lanes : lanes + pairs] * gain
    for off in range(1, n_lane):
        block = fin.at[rows_of((me + n_lane - off) % n_lane), :]
        remote(block, block, send_f.at[off], recv_f.at[off], {"lane": sibling}).wait_recv()
    placed = jnp.zeros((pairs, 128), F32)
    for part in pieces(fin[...], 3):
        placed += nn(place, part)
    back = (iota((lag_dev, 128), 0) == iota((lag_dev, 128), 1)).astype(BF16)
    final = jnp.zeros((lag_dev, pairs), F32)
    for part in pieces(placed, 3):
        final += nt(back, part)
    out_ref[0] = final * gain
    for copy in sent:
        copy.wait_send()


def per_device(waveforms, patterns, partners, counts):
    lane_dev, time_dev = waveforms.shape
    slots = partners.shape[1]
    n_lane, n_rec = lax.axis_size("lane"), lax.axis_size("rec")
    lanes, pairs = lane_dev * n_lane, lane_dev * slots
    n_z = n_lane // 2
    lag_dev = LAGS // n_rec
    cols = FINE * lane_dev
    chunks = 4
    scale = (5.0 * time_dev * n_rec) ** -0.5
    meta = jnp.concatenate([partners, counts[:, None]], axis=1)
    meta = jnp.pad(meta, ((0, 0), (0, 128 - slots - 1)))
    dma = pltpu.SemaphoreType.DMA
    return pl.pallas_call(
        functools.partial(kernel, n_lane, n_rec, slots, scale, chunks),
        out_shape=jax.ShapeDtypeStruct((2, lag_dev, pairs), F32),
        in_specs=[pl.BlockSpec(memory_space=pltpu.VMEM)] * 3,
        out_specs=pl.BlockSpec(memory_space=pltpu.VMEM),
        scratch_shapes=[
            pltpu.VMEM((lanes, time_dev), BF16),
            pltpu.VMEM((lanes, 128), jnp.int32),
            pltpu.VMEM((lane_dev, LAGS), BF16),
            pltpu.VMEM((lane_dev, LAGS), BF16),
            pltpu.VMEM((cols, time_dev + LAGS), BF16),
            pltpu.VMEM((time_dev + LAGS, cols), BF16),
            pltpu.VMEM((STEPS, lanes, cols), F32),
            pltpu.VMEM((n_rec, lag_dev, lanes + pairs), F32),
            pltpu.VMEM((n_rec, lag_dev, lanes + pairs), F32),
            pltpu.VMEM((lanes, 128), F32),
            pltpu.VMEM((lanes, 128), F32),
            dma((n_z, chunks)), dma((n_z, chunks)),
            dma((n_z, chunks)), dma((n_z, chunks)),
            dma((n_lane,)), dma((n_lane,)),
            dma((1,)), dma((1,)),
            dma((n_rec,)), dma((n_rec,)),
            dma((n_lane,)), dma((n_lane,)),
        ],
        compiler_params=pltpu.CompilerParams(
            collective_id=0, has_side_effects=True, vmem_limit_bytes=48 * 1024 * 1024
        ),
    )(waveforms, patterns, meta)


def solution(mesh):
    in_specs = (P("lane", "rec"), P("lane", "rec"), P("lane", None), P("lane"))
    out_specs = P(None, "rec", "lane")
    return jax.shard_map(
        per_device, mesh=mesh, in_specs=in_specs, out_specs=out_specs, check_vma=False
    )
```

```python
import functools

import jax
import jax.numpy as jnp
from jax import lax
from jax.experimental import pallas as pl
from jax.experimental.pallas import tpu as pltpu
from jax.sharding import PartitionSpec as P

LAGS = 256
HALF = 128
MESH = pl.DeviceIdType.MESH
F32 = jnp.float32
BF16 = jnp.bfloat16


def nn(a, b):
    return lax.dot_general(a, b, (((1,), (0,)), ((), ())), preferred_element_type=F32)


def nt(a, b):
    return lax.dot_general(a, b, (((1,), (1,)), ((), ())), preferred_element_type=F32)


def pieces(x, count):
    parts = []
    for _ in range(count):
        part = x.astype(BF16)
        parts.append(part)
        x = x - part.astype(F32)
    return parts


def iota(shape, axis):
    return lax.broadcasted_iota(jnp.int32, shape, axis)


def spread_out(values, where):
    low, high = values % 64, values // 64
    low, high = low.astype(F32).astype(BF16), high.astype(F32).astype(BF16)
    return 64.0 * nn(high, where) + nn(low, where)


def kernel(
    n_lane, n_rec, scale, chunks,
    w_ref, pat_ref, partners_ref, counts_ref, out_ref,
    wall, pats, ext, named, rim, halo, delayed, acc, zbuf, zin, fout, fin,
    local_w, local_p, send_d, recv_d, send_s, recv_s, send_m, recv_m, send_h, recv_h,
    send_z, recv_z, send_f, recv_f,
):
    lane_dev, time_dev = w_ref.shape
    slots = partners_ref.shape[0]
    lanes = lane_dev * n_lane
    pairs = lane_dev * slots
    n_z = n_lane // 2
    lag_dev = LAGS // n_rec
    wide = time_dev // chunks
    me = lax.axis_index("lane")
    rec = lax.axis_index("rec")
    z, core = me // 2, me % 2
    sibling = 2 * z + 1 - core

    barrier = pltpu.get_barrier_semaphore()
    for off in range(1, n_lane):
        pl.semaphore_signal(
            barrier, inc=1, device_id={"lane": (me + off) % n_lane}, device_id_type=MESH
        )
    for off in range(1, n_rec):
        pl.semaphore_signal(
            barrier, inc=1, device_id={"rec": (rec + off) % n_rec}, device_id_type=MESH
        )

    def rows_of(owner):
        return pl.ds(pl.multiple_of(owner * lane_dev, lane_dev), lane_dev)

    def remote(src, dst, send, recv, where):
        return pltpu.make_async_remote_copy(
            src_ref=src, dst_ref=dst, send_sem=send, recv_sem=recv,
            device_id=where, device_id_type=MESH,
        )

    def span(c):
        return pl.ds(HALF + c * wide, wide)

    def from_chip(off, same):
        return rows_of(2 * ((z + n_z - off) % n_z) + (core if same else 1 - core))

    take_p = pltpu.make_async_copy(pat_ref, pats, local_p.at[0])
    take_p.start()
    take_w = pltpu.make_async_copy(
        w_ref, wall.at[rows_of(me), pl.ds(HALF, time_dev)], local_w.at[0]
    )
    take_w.start()
    edge = jnp.zeros((lanes, HALF), BF16)
    wall[:, 0:HALF] = edge
    wall[:, HALF + time_dev : 2 * HALF + time_dev] = edge
    spot = (iota((lane_dev, lanes), 0) + me * lane_dev == iota((lane_dev, lanes), 1)).astype(BF16)
    inside = spread_out(partners_ref[...] + 1, spot)
    named[0] = inside
    take_p.wait()
    levels = (2 * pats[...] - 3).astype(F32)
    ext[:, LAGS : LAGS + time_dev] = levels
    rim[...] = levels[:, time_dev - LAGS :].astype(BF16)

    pl.semaphore_wait(barrier, n_lane - 1 + n_rec - 1)

    sent = []

    def go(copy):
        copy.start()
        sent.append(copy)

    to_next = remote(rim, halo, send_h.at[0], recv_h.at[0], {"rec": (rec + 1) % n_rec})
    go(to_next)
    for c in range(chunks):
        part = w_ref.at[:, pl.ds(c * wide, wide)]
        for off in range(1, n_z):
            go(
                remote(
                    part, wall.at[rows_of(me), span(c)], send_d.at[off, c], recv_d.at[off, c],
                    {"lane": 2 * ((z + off) % n_z) + core},
                )
            )
        go(
            remote(
                part, wall.at[rows_of(me), span(c)], send_s.at[0, c], recv_s.at[0, c],
                {"lane": sibling},
            )
        )
    for off in range(1, n_lane):
        go(
            remote(
                named.at[0], named.at[off], send_m.at[off], recv_m.at[off],
                {"lane": (me + off) % n_lane},
            )
        )

    to_next.wait_recv()
    ext[:, 0:LAGS] = jnp.where(rec > 0, halo[...].astype(F32), 0.0)

    def width_of(c):
        return wide + (HALF if c == chunks - 1 else 0)

    def delay(c):
        def body(m, carry):
            row = ext[pl.ds(m, 1), c * wide : c * wide + width_of(c) + HALF]
            same = jnp.broadcast_to(row, (HALF, width_of(c) + HALF))
            moved = pltpu.roll(same, 0, 1, stride=1, stride_axis=0)
            delayed[pl.ds(pl.multiple_of(m * HALF, HALF), HALF), c * wide : c * wide + width_of(c)] = (
                moved[:, HALF:].astype(BF16)
            )
            return carry

        lax.fori_loop(0, lane_dev, body, 0)

    group = 4

    def multiply(c):
        def body(g, carry):
            first = wall[:, c * wide : c * wide + width_of(c)]
            second = wall[:, c * wide + HALF : c * wide + width_of(c) + HALF]
            held = jnp.concatenate([first, second], axis=0)
            rows = pl.ds(pl.multiple_of(g * group * HALF, group * HALF), group * HALF)
            term = nt(delayed[rows, c * wide : c * wide + width_of(c)], held)
            if c == 0:
                acc[rows, :] = term
            else:
                acc[rows, :] += term
            return carry

        lax.fori_loop(0, lane_dev // group, body, 0)

    for c in range(chunks + 1):
        if c < chunks:
            delay(c)
            for off in range(1, n_z):
                block = wall.at[from_chip(off, True), span(c)]
                remote(
                    block, block, send_d.at[off, c], recv_d.at[off, c], {"lane": sibling}
                ).wait_recv()
                go(remote(block, block, send_s.at[off, c], recv_s.at[off, c], {"lane": sibling}))
        if c == 1:
            take_w.wait()
        if c > 0:
            for off in range(n_z):
                block = wall.at[from_chip(off, False), span(c - 1)]
                remote(
                    block, block, send_s.at[off, c - 1], recv_s.at[off, c - 1], {"lane": sibling}
                ).wait_recv()
            multiply(c - 1)

    for off in range(1, n_lane):
        remote(
            named.at[off], named.at[off], send_m.at[off], recv_m.at[off], {"lane": sibling}
        ).wait_recv()
        inside = inside + named[off]
    local = inside - 1.0 - (me * lane_dev).astype(F32)
    here = (local >= 0.0) & (local < float(lane_dev))
    mine = jnp.sum(jnp.where(here, local + 1.0, 0.0), axis=0, keepdims=True) - 1.0
    pair_of = iota((lane_dev, pairs), 1)
    owner = (pair_of // slots == iota((lane_dev, pairs), 0)).astype(BF16)
    tall = spread_out(partners_ref[...], owner)
    at_slot = iota((slots, pairs), 1) % slots == iota((slots, pairs), 0)
    target = jnp.sum(jnp.where(at_slot, tall, 0.0), axis=0, keepdims=True).astype(jnp.int32)
    pair_row = iota((1, pairs), 1)
    pick = (target == iota((lanes, pairs), 0)).astype(BF16)
    place = (
        (target // lane_dev) * lane_dev + pair_row // slots == iota((lanes, pairs), 0)
    ).astype(BF16)
    counted = nn(
        jnp.broadcast_to(counts_ref[...], (8, lane_dev)).astype(F32).astype(BF16), owner
    )[0:1]
    gain = jnp.where((pair_row % slots).astype(F32) < counted, F32(scale), 0.0)

    for off in list(range(1, n_rec)) + [0]:
        there = (rec + off) % n_rec
        first = there * lag_dev
        across = pl.ds(pl.multiple_of((first // HALF) * lanes, lanes), lanes)
        delay_at = first % HALF
        forward = jnp.zeros((lag_dev, lanes), F32)
        stack = []
        for m in range(lane_dev):
            rows = pl.ds(pl.multiple_of(m * HALF + delay_at, lag_dev), lag_dev)
            block = acc[rows, across]
            forward = jnp.where(mine == float(m), block, forward)
            stack.extend(pieces(block, 2))
        picked = nn(jnp.concatenate(stack, axis=0), pick)
        reverse = jnp.zeros((lag_dev, pairs), F32)
        for m in range(lane_dev):
            at = 2 * m * lag_dev
            both = picked[at : at + lag_dev] + picked[at + lag_dev : at + 2 * lag_dev]
            reverse = jnp.where(pair_row // slots == m, both, reverse)
        zbuf[off, :, 0:lanes] = forward
        zbuf[off, :, lanes : lanes + pairs] = reverse
        if off > 0:
            go(remote(zbuf.at[off], zin.at[off], send_z.at[off], recv_z.at[off], {"rec": there}))

    total = zbuf[0]
    for off in range(1, n_rec):
        remote(
            zbuf.at[off], zin.at[off], send_z.at[off], recv_z.at[off], {"lane": sibling}
        ).wait_recv()
        total += zin[off]

    line = (iota((lanes, lanes), 0) == iota((lanes, lanes), 1)).astype(BF16)
    forward_sum = total[:, 0:lanes]
    if lag_dev < 128:
        forward_sum = jnp.concatenate(
            [forward_sum, jnp.zeros((128 - lag_dev, lanes), F32)], axis=0
        )
    turned = jnp.zeros((lanes, 128), F32)
    for part in pieces(forward_sum, 3):
        turned += nt(line, part)
    fout[...] = turned
    fin[rows_of(me), :] = fout[rows_of(me), :]
    for off in range(1, n_lane):
        there = (me + off) % n_lane
        go(
            remote(
                fout.at[rows_of(there), :], fin.at[rows_of(me), :],
                send_f.at[off], recv_f.at[off], {"lane": there},
            )
        )
    out_ref[1] = total[:, lanes : lanes + pairs] * gain
    for off in range(1, n_lane):
        block = fin.at[rows_of((me + n_lane - off) % n_lane), :]
        remote(block, block, send_f.at[off], recv_f.at[off], {"lane": sibling}).wait_recv()
    back = (iota((lag_dev, 128), 0) == iota((lag_dev, 128), 1)).astype(BF16)
    final = jnp.zeros((lag_dev, pairs), F32)
    for part in pieces(fin[...], 3):
        final += nn(nt(back, part).astype(BF16), place)
    out_ref[0] = final * gain
    for copy in sent:
        copy.wait_send()


def per_device(waveforms, patterns, partners, counts):
    lane_dev, time_dev = waveforms.shape
    slots = partners.shape[1]
    n_lane, n_rec = lax.axis_size("lane"), lax.axis_size("rec")
    lanes, pairs = lane_dev * n_lane, lane_dev * slots
    n_z = n_lane // 2
    lag_dev = LAGS // n_rec
    chunks = 4
    scale = (5.0 * time_dev * n_rec) ** -0.5
    dma = pltpu.SemaphoreType.DMA
    return pl.pallas_call(
        functools.partial(kernel, n_lane, n_rec, scale, chunks),
        out_shape=jax.ShapeDtypeStruct((2, lag_dev, pairs), F32),
        in_specs=[pl.BlockSpec(memory_space=pltpu.HBM)] * 2
        + [pl.BlockSpec(memory_space=pltpu.VMEM)] * 2,
        out_specs=pl.BlockSpec(memory_space=pltpu.VMEM),
        scratch_shapes=[
            pltpu.VMEM((lanes, time_dev + 2 * HALF), BF16),
            pltpu.VMEM((lane_dev, time_dev), jnp.int32),
            pltpu.VMEM((lane_dev, time_dev + LAGS), F32),
            pltpu.VMEM((n_lane, slots, lanes), F32),
            pltpu.VMEM((lane_dev, LAGS), BF16),
            pltpu.VMEM((lane_dev, LAGS), BF16),
            pltpu.VMEM((lane_dev * HALF, time_dev + HALF), BF16),
            pltpu.VMEM((lane_dev * HALF, 2 * lanes), F32),
            pltpu.VMEM((n_rec, lag_dev, lanes + pairs), F32),
            pltpu.VMEM((n_rec, lag_dev, lanes + pairs), F32),
            pltpu.VMEM((lanes, 128), F32),
            pltpu.VMEM((lanes, 128), F32),
            dma((1,)), dma((1,)),
            dma((n_z, chunks)), dma((n_z, chunks)),
            dma((n_z, chunks)), dma((n_z, chunks)),
            dma((n_lane,)), dma((n_lane,)),
            dma((1,)), dma((1,)),
            dma((n_rec,)), dma((n_rec,)),
            dma((n_lane,)), dma((n_lane,)),
        ],
        compiler_params=pltpu.CompilerParams(
            collective_id=0, has_side_effects=True, vmem_limit_bytes=56 * 1024 * 1024
        ),
    )(waveforms, patterns, partners.T, counts[None, :])


def solution(mesh):
    in_specs = (P("lane", "rec"), P("lane", "rec"), P("lane", None), P("lane"))
    out_specs = P(None, "rec", "lane")
    return jax.shard_map(
        per_device, mesh=mesh, in_specs=in_specs, out_specs=out_specs, check_vma=False
    )
```

```python
import functools

import jax
import jax.numpy as jnp
from jax import lax
from jax.experimental import pallas as pl
from jax.experimental.pallas import tpu as pltpu
from jax.sharding import PartitionSpec as P

LAGS = 256
HALF = 128
FINE = 16
STEPS = HALF // FINE
MESH = pl.DeviceIdType.MESH
F32 = jnp.float32
BF16 = jnp.bfloat16


def nn(a, b):
    return lax.dot_general(a, b, (((1,), (0,)), ((), ())), preferred_element_type=F32)


def nt(a, b):
    return lax.dot_general(a, b, (((1,), (1,)), ((), ())), preferred_element_type=F32)


def pieces(x, count):
    parts = []
    for _ in range(count):
        part = x.astype(BF16)
        parts.append(part)
        x = x - part.astype(F32)
    return parts


def iota(shape, axis):
    return lax.broadcasted_iota(jnp.int32, shape, axis)


def spread_out(values, where):
    low, high = values % 64, values // 64
    low, high = low.astype(F32).astype(BF16), high.astype(F32).astype(BF16)
    return 64.0 * nn(high, where) + nn(low, where)


def kernel(
    n_lane, n_rec, scale, chunks,
    w_ref, pat_ref, partners_ref, counts_ref, out_ref,
    wall, pats, named, rim, halo, shifted, refs, acc, zbuf, zin, fout, fin,
    local_w, local_p, send_d, recv_d, send_s, recv_s, send_m, recv_m, send_h, recv_h,
    send_z, recv_z, send_f, recv_f,
):
    lane_dev, time_dev = w_ref.shape
    slots = partners_ref.shape[0]
    lanes = lane_dev * n_lane
    pairs = lane_dev * slots
    n_z = n_lane // 2
    lag_dev = LAGS // n_rec
    wide = time_dev // chunks
    cols = FINE * lane_dev
    me = lax.axis_index("lane")
    rec = lax.axis_index("rec")
    z, core = me // 2, me % 2
    sibling = 2 * z + 1 - core

    barrier = pltpu.get_barrier_semaphore()
    for off in range(1, n_lane):
        pl.semaphore_signal(
            barrier, inc=1, device_id={"lane": (me + off) % n_lane}, device_id_type=MESH
        )
    for off in range(1, n_rec):
        pl.semaphore_signal(
            barrier, inc=1, device_id={"rec": (rec + off) % n_rec}, device_id_type=MESH
        )

    def rows_of(owner):
        return pl.ds(pl.multiple_of(owner * lane_dev, lane_dev), lane_dev)

    def remote(src, dst, send, recv, where):
        return pltpu.make_async_remote_copy(
            src_ref=src, dst_ref=dst, send_sem=send, recv_sem=recv,
            device_id=where, device_id_type=MESH,
        )

    def span(c):
        return pl.ds(HALF + c * wide, wide)

    def from_chip(off, same):
        return rows_of(2 * ((z + n_z - off) % n_z) + (core if same else 1 - core))

    take_p = pltpu.make_async_copy(pat_ref, pats, local_p.at[0])
    take_p.start()
    take_w = pltpu.make_async_copy(
        w_ref, wall.at[rows_of(me), pl.ds(HALF, time_dev)], local_w.at[0]
    )
    take_w.start()
    edge = jnp.zeros((lanes, HALF), BF16)
    wall[:, 0:HALF] = edge
    wall[:, HALF + time_dev : 2 * HALF + time_dev] = edge
    spot = (iota((lane_dev, lanes), 0) + me * lane_dev == iota((lane_dev, lanes), 1)).astype(BF16)
    inside = spread_out(partners_ref[...] + 1, spot)
    named[0] = inside
    take_p.wait()
    levels = (2 * pats[...] - 3).astype(F32)
    rim[...] = levels[:, time_dev - LAGS :].astype(BF16)

    pl.semaphore_wait(barrier, n_lane - 1 + n_rec - 1)

    sent = []

    def go(copy):
        copy.start()
        sent.append(copy)

    to_next = remote(rim, halo, send_h.at[0], recv_h.at[0], {"rec": (rec + 1) % n_rec})
    go(to_next)
    for c in range(chunks):
        part = w_ref.at[:, pl.ds(c * wide, wide)]
        for off in range(1, n_z):
            go(
                remote(
                    part, wall.at[rows_of(me), span(c)], send_d.at[off, c], recv_d.at[off, c],
                    {"lane": 2 * ((z + off) % n_z) + core},
                )
            )
        go(
            remote(
                part, wall.at[rows_of(me), span(c)], send_s.at[0, c], recv_s.at[0, c],
                {"lane": sibling},
            )
        )
    for off in range(1, n_lane):
        go(
            remote(
                named.at[0], named.at[off], send_m.at[off], recv_m.at[off],
                {"lane": (me + off) % n_lane},
            )
        )

    unit = (iota((LAGS, LAGS), 0) == iota((LAGS, LAGS), 1)).astype(BF16)

    def turn(b):
        part = slice(b * LAGS, (b + 1) * LAGS)
        refs[part, :] = nt(unit, shifted[:, part]).astype(BF16)

    for r in range(FINE):
        moved = levels if r == 0 else pltpu.roll(levels, r, 1)
        shifted[r * lane_dev : (r + 1) * lane_dev, LAGS:] = moved.astype(BF16)
    for b in range(2, time_dev // LAGS + 1):
        turn(b)
    to_next.wait_recv()
    before = jnp.where(rec > 0, halo[...].astype(F32), 0.0)
    rest = jnp.concatenate([before, levels[:, 0:LAGS]], axis=1)
    for r in range(FINE):
        moved = rest if r == 0 else pltpu.roll(rest, r, 1)
        shifted[r * lane_dev : (r + 1) * lane_dev, 0 : 2 * LAGS] = moved.astype(BF16)
    for b in range(2):
        turn(b)

    def multiply(c):
        begin = c * wide
        width = wide + (HALF if c == chunks - 1 else 0)
        group = 2

        def body(step, carry):
            first = wall[:, begin : begin + width]
            second = wall[:, begin + HALF : begin + HALF + width]
            rows = jnp.concatenate([first, second], axis=0)
            for i in range(group):
                a = step * group + i
                start = pl.multiple_of(begin + HALF - FINE * a, FINE)
                term = nn(rows, refs[pl.ds(start, width), :])
                if c == 0:
                    acc[a] = term
                else:
                    acc[a] += term
            return carry

        lax.fori_loop(0, STEPS // group, body, 0)

    for c in range(chunks + 1):
        if c < chunks:
            for off in range(1, n_z):
                block = wall.at[from_chip(off, True), span(c)]
                remote(
                    block, block, send_d.at[off, c], recv_d.at[off, c], {"lane": sibling}
                ).wait_recv()
                go(remote(block, block, send_s.at[off, c], recv_s.at[off, c], {"lane": sibling}))
        if c == 1:
            take_w.wait()
        if c > 0:
            for off in range(n_z):
                block = wall.at[from_chip(off, False), span(c - 1)]
                remote(
                    block, block, send_s.at[off, c - 1], recv_s.at[off, c - 1], {"lane": sibling}
                ).wait_recv()
            multiply(c - 1)

    for off in range(1, n_lane):
        remote(
            named.at[off], named.at[off], send_m.at[off], recv_m.at[off], {"lane": sibling}
        ).wait_recv()
        inside = inside + named[off]
    local = inside - 1.0 - (me * lane_dev).astype(F32)
    here = (local >= 0.0) & (local < float(lane_dev))
    keep = jnp.where(here, local + 1.0, 0.0)

    def turn_small(rows):
        width = rows.shape[1]
        same = (iota((width, width), 0) == iota((width, width), 1)).astype(BF16)
        low, high = rows.astype(jnp.int32) % 64, rows.astype(jnp.int32) // 64
        low, high = low.astype(F32).astype(BF16), high.astype(F32).astype(BF16)
        column = jnp.sum(64.0 * nt(same, high) + nt(same, low), axis=1, keepdims=True)
        return column.astype(jnp.int32)

    mine = turn_small(keep) - 1
    keep_forward = iota((lanes, cols), 1) % lane_dev == mine
    pair_of = iota((lane_dev, pairs), 1)
    owner = (pair_of // slots == iota((lane_dev, pairs), 0)).astype(BF16)
    tall = spread_out(partners_ref[...], owner)
    at_slot = iota((slots, pairs), 1) % slots == iota((slots, pairs), 0)
    target = jnp.sum(jnp.where(at_slot, tall, 0.0), axis=0, keepdims=True).astype(jnp.int32)
    pair_row = iota((1, pairs), 1)
    tall_column = turn_small(jnp.where(at_slot, tall, 0.0))
    pick = (tall_column == iota((pairs, lanes), 1)).astype(BF16)
    pick = jnp.concatenate([pick, pick], axis=1)
    keep_reverse = iota((pairs, cols), 1) % lane_dev == iota((pairs, cols), 0) // slots
    gather = (iota((FINE, cols), 1) // lane_dev == iota((FINE, cols), 0)).astype(BF16)
    place = (
        (target // lane_dev) * lane_dev + pair_row // slots == iota((lanes, pairs), 0)
    ).astype(BF16)
    counted = nn(
        jnp.broadcast_to(counts_ref[...], (8, lane_dev)).astype(F32).astype(BF16), owner
    )[0:1]
    gain = jnp.where((pair_row % slots).astype(F32) < counted, F32(scale), 0.0)

    for off in list(range(1, n_rec)) + [0]:
        there = (rec + off) % n_rec
        count = lag_dev // FINE
        first = there * count
        rows = pl.ds(pl.multiple_of((first // STEPS) * lanes, lanes), lanes)
        blocks = [acc[first % STEPS + i, rows, :] for i in range(count)]
        kept = [jnp.where(keep_forward, block, 0.0) for block in blocks]
        split = [jnp.concatenate(pieces(block, 2), axis=0) for block in blocks]
        picked = nn(pick, jnp.concatenate(split, axis=1))
        for i in range(count):
            kept.append(jnp.where(keep_reverse, picked[:, i * cols : (i + 1) * cols], 0.0))
        kept = jnp.concatenate(kept, axis=0)
        summed = jnp.zeros((FINE, kept.shape[0]), F32)
        for part in pieces(kept, 2):
            summed += nt(gather, part)
        for i in range(count):
            at = slice(i * FINE, (i + 1) * FINE)
            zbuf[off, at, 0:lanes] = summed[:, i * lanes : (i + 1) * lanes]
            begin = count * lanes + i * pairs
            zbuf[off, at, lanes : lanes + pairs] = summed[:, begin : begin + pairs]
        if off > 0:
            go(remote(zbuf.at[off], zin.at[off], send_z.at[off], recv_z.at[off], {"rec": there}))

    total = zbuf[0]
    for off in range(1, n_rec):
        remote(
            zbuf.at[off], zin.at[off], send_z.at[off], recv_z.at[off], {"lane": sibling}
        ).wait_recv()
        total += zin[off]

    line = (iota((lanes, lanes), 0) == iota((lanes, lanes), 1)).astype(BF16)
    forward_sum = total[:, 0:lanes]
    if lag_dev < 128:
        forward_sum = jnp.concatenate(
            [forward_sum, jnp.zeros((128 - lag_dev, lanes), F32)], axis=0
        )
    turned = jnp.zeros((lanes, 128), F32)
    for part in pieces(forward_sum, 3):
        turned += nt(line, part)
    fout[...] = turned
    fin[rows_of(me), :] = fout[rows_of(me), :]
    for off in range(1, n_lane):
        there = (me + off) % n_lane
        go(
            remote(
                fout.at[rows_of(there), :], fin.at[rows_of(me), :],
                send_f.at[off], recv_f.at[off], {"lane": there},
            )
        )
    out_ref[1] = total[:, lanes : lanes + pairs] * gain
    for off in range(1, n_lane):
        block = fin.at[rows_of((me + n_lane - off) % n_lane), :]
        remote(block, block, send_f.at[off], recv_f.at[off], {"lane": sibling}).wait_recv()
    back = (iota((lag_dev, 128), 0) == iota((lag_dev, 128), 1)).astype(BF16)
    final = jnp.zeros((lag_dev, pairs), F32)
    for part in pieces(fin[...], 3):
        final += nn(nt(back, part).astype(BF16), place)
    out_ref[0] = final * gain
    for copy in sent:
        copy.wait_send()


def per_device(waveforms, patterns, partners, counts):
    lane_dev, time_dev = waveforms.shape
    slots = partners.shape[1]
    n_lane, n_rec = lax.axis_size("lane"), lax.axis_size("rec")
    lanes, pairs = lane_dev * n_lane, lane_dev * slots
    n_z = n_lane // 2
    lag_dev = LAGS // n_rec
    cols = FINE * lane_dev
    chunks = 4
    scale = (5.0 * time_dev * n_rec) ** -0.5
    dma = pltpu.SemaphoreType.DMA
    return pl.pallas_call(
        functools.partial(kernel, n_lane, n_rec, scale, chunks),
        out_shape=jax.ShapeDtypeStruct((2, lag_dev, pairs), F32),
        in_specs=[pl.BlockSpec(memory_space=pltpu.HBM)] * 2
        + [pl.BlockSpec(memory_space=pltpu.VMEM)] * 2,
        out_specs=pl.BlockSpec(memory_space=pltpu.VMEM),
        scratch_shapes=[
            pltpu.VMEM((lanes, time_dev + 2 * HALF), BF16),
            pltpu.VMEM((lane_dev, time_dev), jnp.int32),
            pltpu.VMEM((n_lane, slots, lanes), F32),
            pltpu.VMEM((lane_dev, LAGS), BF16),
            pltpu.VMEM((lane_dev, LAGS), BF16),
            pltpu.VMEM((cols, time_dev + LAGS), BF16),
            pltpu.VMEM((time_dev + LAGS, cols), BF16),
            pltpu.VMEM((STEPS, 2 * lanes, cols), F32),
            pltpu.VMEM((n_rec, lag_dev, lanes + pairs), F32),
            pltpu.VMEM((n_rec, lag_dev, lanes + pairs), F32),
            pltpu.VMEM((lanes, 128), F32),
            pltpu.VMEM((lanes, 128), F32),
            dma((1,)), dma((1,)),
            dma((n_z, chunks)), dma((n_z, chunks)),
            dma((n_z, chunks)), dma((n_z, chunks)),
            dma((n_lane,)), dma((n_lane,)),
            dma((1,)), dma((1,)),
            dma((n_rec,)), dma((n_rec,)),
            dma((n_lane,)), dma((n_lane,)),
        ],
        compiler_params=pltpu.CompilerParams(
            collective_id=0, has_side_effects=True, vmem_limit_bytes=56 * 1024 * 1024
        ),
    )(waveforms, patterns, partners.T, counts[None, :])


def solution(mesh):
    in_specs = (P("lane", "rec"), P("lane", "rec"), P("lane", None), P("lane"))
    out_specs = P(None, "rec", "lane")
    return jax.shard_map(
        per_device, mesh=mesh, in_specs=in_specs, out_specs=out_specs, check_vma=False
    )
```

```python
import functools

import jax
import jax.numpy as jnp
from jax import lax
from jax.experimental import pallas as pl
from jax.experimental.pallas import tpu as pltpu
from jax.sharding import PartitionSpec as P

LAGS = 256
HALF = 128
FINE = 16
STEPS = HALF // FINE
MESH = pl.DeviceIdType.MESH
F32 = jnp.float32
BF16 = jnp.bfloat16


def nn(a, b):
    return lax.dot_general(a, b, (((1,), (0,)), ((), ())), preferred_element_type=F32)


def nt(a, b):
    return lax.dot_general(a, b, (((1,), (1,)), ((), ())), preferred_element_type=F32)


def pieces(x, count):
    parts = []
    for _ in range(count):
        part = x.astype(BF16)
        parts.append(part)
        x = x - part.astype(F32)
    return parts


def iota(shape, axis):
    return lax.broadcasted_iota(jnp.int32, shape, axis)


def spread_out(values, where):
    low, high = values % 64, values // 64
    low, high = low.astype(F32).astype(BF16), high.astype(F32).astype(BF16)
    return 64.0 * nn(high, where) + nn(low, where)


def kernel(
    n_lane, n_rec, scale, chunks,
    w_ref, pat_ref, partners_ref, counts_ref, out_ref,
    wall, pats, named, rim, halo, shifted, refs, acc, zbuf, zin, fout, fin,
    local_w, local_p, send_d, recv_d, send_s, recv_s, send_m, recv_m, send_h, recv_h,
    send_z, recv_z, send_f, recv_f,
):
    lane_dev, time_dev = w_ref.shape
    slots = partners_ref.shape[0]
    lanes = lane_dev * n_lane
    pairs = lane_dev * slots
    n_z = n_lane // 2
    lag_dev = LAGS // n_rec
    wide = time_dev // chunks
    cols = FINE * lane_dev
    me = lax.axis_index("lane")
    rec = lax.axis_index("rec")
    z, core = me // 2, me % 2
    sibling = 2 * z + 1 - core

    barrier = pltpu.get_barrier_semaphore()
    for off in range(1, n_lane):
        pl.semaphore_signal(
            barrier, inc=1, device_id={"lane": (me + off) % n_lane}, device_id_type=MESH
        )
    for off in range(1, n_rec):
        pl.semaphore_signal(
            barrier, inc=1, device_id={"rec": (rec + off) % n_rec}, device_id_type=MESH
        )

    def rows_of(owner):
        return pl.ds(pl.multiple_of(owner * lane_dev, lane_dev), lane_dev)

    def remote(src, dst, send, recv, where):
        return pltpu.make_async_remote_copy(
            src_ref=src, dst_ref=dst, send_sem=send, recv_sem=recv,
            device_id=where, device_id_type=MESH,
        )

    def span(c):
        return pl.ds(HALF + c * wide, wide)

    def from_chip(off, same):
        return rows_of(2 * ((z + n_z - off) % n_z) + (core if same else 1 - core))

    take_p = pltpu.make_async_copy(pat_ref, pats, local_p.at[0])
    take_p.start()
    take_w = pltpu.make_async_copy(
        w_ref, wall.at[rows_of(me), pl.ds(HALF, time_dev)], local_w.at[0]
    )
    take_w.start()
    edge = jnp.zeros((lanes, HALF), BF16)
    wall[:, 0:HALF] = edge
    wall[:, HALF + time_dev : 2 * HALF + time_dev] = edge
    spot = (iota((lane_dev, lanes), 0) + me * lane_dev == iota((lane_dev, lanes), 1)).astype(BF16)
    inside = spread_out(partners_ref[...] + 1, spot)
    named[0] = inside
    take_p.wait()
    levels = (2 * pats[...] - 3).astype(F32)
    rim[...] = levels[:, time_dev - LAGS :].astype(BF16)

    pl.semaphore_wait(barrier, n_lane - 1 + n_rec - 1)

    sent = []

    def go(copy):
        copy.start()
        sent.append(copy)

    to_next = remote(rim, halo, send_h.at[0], recv_h.at[0], {"rec": (rec + 1) % n_rec})
    go(to_next)
    for off in range(1, n_lane):
        go(
            remote(
                named.at[0], named.at[off], send_m.at[off], recv_m.at[off],
                {"lane": (me + off) % n_lane},
            )
        )
    for c in range(chunks):
        part = w_ref.at[:, pl.ds(c * wide, wide)]
        for off in range(1, n_z):
            go(
                remote(
                    part, wall.at[rows_of(me), span(c)], send_d.at[off, c], recv_d.at[off, c],
                    {"lane": 2 * ((z + off) % n_z) + core},
                )
            )
        go(
            remote(
                part, wall.at[rows_of(me), span(c)], send_s.at[0, c], recv_s.at[0, c],
                {"lane": sibling},
            )
        )
    unit = (iota((LAGS, LAGS), 0) == iota((LAGS, LAGS), 1)).astype(BF16)

    def turn(b):
        part = slice(b * LAGS, (b + 1) * LAGS)
        refs[part, :] = nt(unit, shifted[:, part]).astype(BF16)

    for r in range(FINE):
        moved = levels if r == 0 else pltpu.roll(levels, r, 1)
        shifted[r * lane_dev : (r + 1) * lane_dev, LAGS:] = moved.astype(BF16)
    for b in range(2, time_dev // LAGS + 1):
        turn(b)
    to_next.wait_recv()
    before = jnp.where(rec > 0, halo[...].astype(F32), 0.0)
    rest = jnp.concatenate([before, levels[:, 0:LAGS]], axis=1)
    for r in range(FINE):
        moved = rest if r == 0 else pltpu.roll(rest, r, 1)
        shifted[r * lane_dev : (r + 1) * lane_dev, 0 : 2 * LAGS] = moved.astype(BF16)
    for b in range(2):
        turn(b)

    for off in range(1, n_lane):
        remote(
            named.at[off], named.at[off], send_m.at[off], recv_m.at[off], {"lane": sibling}
        ).wait_recv()
        inside = inside + named[off]
    local = inside - 1.0 - (me * lane_dev).astype(F32)
    here = (local >= 0.0) & (local < float(lane_dev))
    keep = jnp.where(here, local + 1.0, 0.0)

    def turn_small(rows):
        width = rows.shape[1]
        same = (iota((width, width), 0) == iota((width, width), 1)).astype(BF16)
        low, high = rows.astype(jnp.int32) % 64, rows.astype(jnp.int32) // 64
        low, high = low.astype(F32).astype(BF16), high.astype(F32).astype(BF16)
        column = jnp.sum(64.0 * nt(same, high) + nt(same, low), axis=1, keepdims=True)
        return column.astype(jnp.int32)

    mine = turn_small(keep) - 1
    keep_forward = iota((lanes, cols), 1) % lane_dev == mine
    pair_of = iota((lane_dev, pairs), 1)
    owner = (pair_of // slots == iota((lane_dev, pairs), 0)).astype(BF16)
    tall = spread_out(partners_ref[...], owner)
    at_slot = iota((slots, pairs), 1) % slots == iota((slots, pairs), 0)
    target = jnp.sum(jnp.where(at_slot, tall, 0.0), axis=0, keepdims=True).astype(jnp.int32)
    pair_row = iota((1, pairs), 1)
    tall_column = turn_small(jnp.where(at_slot, tall, 0.0))
    pick = (tall_column == iota((pairs, lanes), 1)).astype(BF16)
    pick = jnp.concatenate([pick, pick], axis=1)
    keep_reverse = iota((pairs, cols), 1) % lane_dev == iota((pairs, cols), 0) // slots
    gather = (iota((FINE, cols), 1) // lane_dev == iota((FINE, cols), 0)).astype(BF16)
    place = (
        (target // lane_dev) * lane_dev + pair_row // slots == iota((lanes, pairs), 0)
    ).astype(BF16)
    counted = nn(
        jnp.broadcast_to(counts_ref[...], (8, lane_dev)).astype(F32).astype(BF16), owner
    )[0:1]
    gain = jnp.where((pair_row % slots).astype(F32) < counted, F32(scale), 0.0)

    def multiply(c):
        begin = c * wide
        width = wide + (HALF if c == chunks - 1 else 0)
        group = 2

        def body(step, carry):
            first = wall[:, begin : begin + width]
            second = wall[:, begin + HALF : begin + HALF + width]
            rows = jnp.concatenate([first, second], axis=0)
            for i in range(group):
                a = step * group + i
                start = pl.multiple_of(begin + HALF - FINE * a, FINE)
                term = nn(rows, refs[pl.ds(start, width), :])
                if c == 0:
                    acc[a] = term
                else:
                    acc[a] += term
            return carry

        lax.fori_loop(0, STEPS // group, body, 0)

    for c in range(chunks + 1):
        if c < chunks:
            for off in range(1, n_z):
                block = wall.at[from_chip(off, True), span(c)]
                remote(
                    block, block, send_d.at[off, c], recv_d.at[off, c], {"lane": sibling}
                ).wait_recv()
                go(remote(block, block, send_s.at[off, c], recv_s.at[off, c], {"lane": sibling}))
        if c == 1:
            take_w.wait()
        if c > 0:
            for off in range(n_z):
                block = wall.at[from_chip(off, False), span(c - 1)]
                remote(
                    block, block, send_s.at[off, c - 1], recv_s.at[off, c - 1], {"lane": sibling}
                ).wait_recv()
            multiply(c - 1)

    for off in list(range(1, n_rec)) + [0]:
        there = (rec + off) % n_rec
        count = lag_dev // FINE
        first = there * count
        rows = pl.ds(pl.multiple_of((first // STEPS) * lanes, lanes), lanes)
        blocks = [acc[first % STEPS + i, rows, :] for i in range(count)]
        kept = [jnp.where(keep_forward, block, 0.0) for block in blocks]
        split = [jnp.concatenate(pieces(block, 2), axis=0) for block in blocks]
        picked = nn(pick, jnp.concatenate(split, axis=1))
        for i in range(count):
            kept.append(jnp.where(keep_reverse, picked[:, i * cols : (i + 1) * cols], 0.0))
        kept = jnp.concatenate(kept, axis=0)
        summed = jnp.zeros((FINE, kept.shape[0]), F32)
        for part in pieces(kept, 2):
            summed += nt(gather, part)
        for i in range(count):
            at = slice(i * FINE, (i + 1) * FINE)
            zbuf[off, at, 0:lanes] = summed[:, i * lanes : (i + 1) * lanes]
            begin = count * lanes + i * pairs
            zbuf[off, at, lanes : lanes + pairs] = summed[:, begin : begin + pairs]
        if off > 0:
            go(remote(zbuf.at[off], zin.at[off], send_z.at[off], recv_z.at[off], {"rec": there}))

    total = zbuf[0]
    for off in range(1, n_rec):
        remote(
            zbuf.at[off], zin.at[off], send_z.at[off], recv_z.at[off], {"lane": sibling}
        ).wait_recv()
        total += zin[off]

    forward_sum = total[:, 0:lanes]
    if lag_dev < 128:
        forward_sum = jnp.concatenate(
            [forward_sum, jnp.zeros((128 - lag_dev, lanes), F32)], axis=0
        )
    fout[...] = forward_sum.T
    fin[rows_of(me), :] = fout[rows_of(me), :]
    for off in range(1, n_lane):
        there = (me + off) % n_lane
        go(
            remote(
                fout.at[rows_of(there), :], fin.at[rows_of(me), :],
                send_f.at[off], recv_f.at[off], {"lane": there},
            )
        )
    out_ref[1] = total[:, lanes : lanes + pairs] * gain
    for off in range(1, n_lane):
        block = fin.at[rows_of((me + n_lane - off) % n_lane), :]
        remote(block, block, send_f.at[off], recv_f.at[off], {"lane": sibling}).wait_recv()
    returned = fin[...].T[0:lag_dev]
    placed = nn(jnp.concatenate(pieces(returned, 3), axis=0), place)
    final = placed[0:lag_dev] + placed[lag_dev : 2 * lag_dev] + placed[2 * lag_dev :]
    out_ref[0] = final * gain
    for copy in sent:
        copy.wait_send()


def per_device(waveforms, patterns, partners, counts):
    lane_dev, time_dev = waveforms.shape
    slots = partners.shape[1]
    n_lane, n_rec = lax.axis_size("lane"), lax.axis_size("rec")
    lanes, pairs = lane_dev * n_lane, lane_dev * slots
    n_z = n_lane // 2
    lag_dev = LAGS // n_rec
    cols = FINE * lane_dev
    chunks = 4
    scale = (5.0 * time_dev * n_rec) ** -0.5
    dma = pltpu.SemaphoreType.DMA
    return pl.pallas_call(
        functools.partial(kernel, n_lane, n_rec, scale, chunks),
        out_shape=jax.ShapeDtypeStruct((2, lag_dev, pairs), F32),
        in_specs=[pl.BlockSpec(memory_space=pltpu.HBM)] * 2
        + [pl.BlockSpec(memory_space=pltpu.VMEM)] * 2,
        out_specs=pl.BlockSpec(memory_space=pltpu.VMEM),
        scratch_shapes=[
            pltpu.VMEM((lanes, time_dev + 2 * HALF), BF16),
            pltpu.VMEM((lane_dev, time_dev), jnp.int32),
            pltpu.VMEM((n_lane, slots, lanes), F32),
            pltpu.VMEM((lane_dev, LAGS), BF16),
            pltpu.VMEM((lane_dev, LAGS), BF16),
            pltpu.VMEM((cols, time_dev + LAGS), BF16),
            pltpu.VMEM((time_dev + LAGS, cols), BF16),
            pltpu.VMEM((STEPS, 2 * lanes, cols), F32),
            pltpu.VMEM((n_rec, lag_dev, lanes + pairs), F32),
            pltpu.VMEM((n_rec, lag_dev, lanes + pairs), F32),
            pltpu.VMEM((lanes, 128), F32),
            pltpu.VMEM((lanes, 128), F32),
            dma((1,)), dma((1,)),
            dma((n_z, chunks)), dma((n_z, chunks)),
            dma((n_z, chunks)), dma((n_z, chunks)),
            dma((n_lane,)), dma((n_lane,)),
            dma((1,)), dma((1,)),
            dma((n_rec,)), dma((n_rec,)),
            dma((n_lane,)), dma((n_lane,)),
        ],
        compiler_params=pltpu.CompilerParams(
            collective_id=0, has_side_effects=True, vmem_limit_bytes=(256 + lanes) * 64 * 1024
        ),
    )(waveforms, patterns, partners.T, counts[None, :])


def solution(mesh):
    in_specs = (P("lane", "rec"), P("lane", "rec"), P("lane", None), P("lane"))
    out_specs = P(None, "rec", "lane")
    return jax.shard_map(
        per_device, mesh=mesh, in_specs=in_specs, out_specs=out_specs, check_vma=False
    )
```

```python
import functools

import jax
import jax.numpy as jnp
from jax import lax
from jax.experimental import pallas as pl
from jax.experimental.pallas import tpu as pltpu
from jax.sharding import PartitionSpec as P

LAGS = 256
HALF = 128
FINE = 16
STEPS = HALF // FINE
MESH = pl.DeviceIdType.MESH
F32 = jnp.float32
BF16 = jnp.bfloat16


def nn(a, b):
    return lax.dot_general(a, b, (((1,), (0,)), ((), ())), preferred_element_type=F32)


def nt(a, b):
    return lax.dot_general(a, b, (((1,), (1,)), ((), ())), preferred_element_type=F32)


def pieces(x, count):
    parts = []
    for _ in range(count):
        part = x.astype(BF16)
        parts.append(part)
        x = x - part.astype(F32)
    return parts


def iota(shape, axis):
    return lax.broadcasted_iota(jnp.int32, shape, axis)


def spread_out(values, where):
    low, high = values % 64, values // 64
    low, high = low.astype(F32).astype(BF16), high.astype(F32).astype(BF16)
    return 64.0 * nn(high, where) + nn(low, where)


def kernel(
    n_lane, n_rec, scale, chunks,
    w_ref, pat_ref, partners_ref, counts_ref, out_ref,
    wall, pats, named, rim, halo, shifted, refs, acc, zbuf, zin, fout, fin,
    local_w, local_p, send_d, recv_d, send_s, recv_s, send_m, recv_m, send_h, recv_h,
    send_z, recv_z, send_f, recv_f,
):
    lane_dev, time_dev = w_ref.shape
    slots = partners_ref.shape[0]
    lanes = lane_dev * n_lane
    pairs = lane_dev * slots
    n_z = n_lane // 2
    lag_dev = LAGS // n_rec
    wide = time_dev // chunks
    cols = FINE * lane_dev
    me = lax.axis_index("lane")
    rec = lax.axis_index("rec")
    z, core = me // 2, me % 2
    sibling = 2 * z + 1 - core

    barrier = pltpu.get_barrier_semaphore()
    for off in range(1, n_lane):
        pl.semaphore_signal(
            barrier, inc=1, device_id={"lane": (me + off) % n_lane}, device_id_type=MESH
        )
    for off in range(1, n_rec):
        pl.semaphore_signal(
            barrier, inc=1, device_id={"rec": (rec + off) % n_rec}, device_id_type=MESH
        )

    def rows_of(owner):
        return pl.ds(pl.multiple_of(owner * lane_dev, lane_dev), lane_dev)

    def remote(src, dst, send, recv, where):
        return pltpu.make_async_remote_copy(
            src_ref=src, dst_ref=dst, send_sem=send, recv_sem=recv,
            device_id=where, device_id_type=MESH,
        )

    def span(c):
        return pl.ds(HALF + c * wide, wide)

    take_p = pltpu.make_async_copy(pat_ref, pats, local_p.at[0])
    take_p.start()
    take_w = pltpu.make_async_copy(
        w_ref, wall.at[rows_of(me), pl.ds(HALF, time_dev)], local_w.at[0]
    )
    take_w.start()
    edge = jnp.zeros((lanes, HALF), BF16)
    wall[:, 0:HALF] = edge
    wall[:, HALF + time_dev : 2 * HALF + time_dev] = edge
    spot = (iota((lane_dev, lanes), 0) + me * lane_dev == iota((lane_dev, lanes), 1)).astype(BF16)
    inside = spread_out(partners_ref[...] + 1, spot)
    named[0] = inside
    take_p.wait()
    levels = (2 * pats[...] - 3).astype(F32)
    rim[...] = levels[:, time_dev - LAGS :].astype(BF16)

    pl.semaphore_wait(barrier, n_lane - 1 + n_rec - 1)

    sent = []

    def go(copy):
        copy.start()
        sent.append(copy)

    to_next = remote(rim, halo, send_h.at[0], recv_h.at[0], {"rec": (rec + 1) % n_rec})
    go(to_next)
    for off in range(1, n_lane):
        go(
            remote(
                named.at[0], named.at[off], send_m.at[off], recv_m.at[off],
                {"lane": (me + off) % n_lane},
            )
        )
    def block_of(chip, same, c):
        owner = 2 * chip + (core if same else 1 - core)
        return wall.at[rows_of(jnp.clip(owner, 0, n_lane - 1)), span(c)]

    def on_line(chip):
        return (chip >= 0) & (chip < n_z)

    def passed(d, side, c, first=False):
        way = 1 - 2 * side
        target = wall.at[rows_of(me), span(c)] if first else block_of(z - way * (d - 1), True, c)
        source = w_ref.at[:, pl.ds(c * wide, wide)] if first else target
        return remote(
            source, target, send_d.at[d, side, c], recv_d.at[d, side, c],
            {"lane": jnp.clip(2 * (z + way) + core, 0, n_lane - 1)},
        )

    def across(d, side, c, same=True):
        block = block_of(z - (1 - 2 * side) * d, same, c)
        return remote(
            block, block, send_s.at[d, side, c], recv_s.at[d, side, c], {"lane": sibling}
        )

    def own_across(c):
        return remote(
            w_ref.at[:, pl.ds(c * wide, wide)], wall.at[rows_of(me), span(c)],
            send_s.at[0, 0, c], recv_s.at[0, 0, c], {"lane": sibling},
        )

    for c in range(chunks):
        for side in range(2):
            @pl.when(on_line(z + 1 - 2 * side))
            def _():
                passed(1, side, c, True).start()
        own_across(c).start()
    unit = (iota((LAGS, LAGS), 0) == iota((LAGS, LAGS), 1)).astype(BF16)

    def turn(b):
        part = slice(b * LAGS, (b + 1) * LAGS)
        refs[part, :] = nt(unit, shifted[:, part]).astype(BF16)

    for r in range(FINE):
        moved = levels if r == 0 else pltpu.roll(levels, r, 1)
        shifted[r * lane_dev : (r + 1) * lane_dev, LAGS:] = moved.astype(BF16)
    for b in range(2, time_dev // LAGS + 1):
        turn(b)
    to_next.wait_recv()
    before = jnp.where(rec > 0, halo[...].astype(F32), 0.0)
    rest = jnp.concatenate([before, levels[:, 0:LAGS]], axis=1)
    for r in range(FINE):
        moved = rest if r == 0 else pltpu.roll(rest, r, 1)
        shifted[r * lane_dev : (r + 1) * lane_dev, 0 : 2 * LAGS] = moved.astype(BF16)
    for b in range(2):
        turn(b)

    for off in range(1, n_lane):
        remote(
            named.at[off], named.at[off], send_m.at[off], recv_m.at[off], {"lane": sibling}
        ).wait_recv()
        inside = inside + named[off]
    local = inside - 1.0 - (me * lane_dev).astype(F32)
    here = (local >= 0.0) & (local < float(lane_dev))
    keep = jnp.where(here, local + 1.0, 0.0)

    def turn_small(rows):
        width = rows.shape[1]
        same = (iota((width, width), 0) == iota((width, width), 1)).astype(BF16)
        low, high = rows.astype(jnp.int32) % 64, rows.astype(jnp.int32) // 64
        low, high = low.astype(F32).astype(BF16), high.astype(F32).astype(BF16)
        column = jnp.sum(64.0 * nt(same, high) + nt(same, low), axis=1, keepdims=True)
        return column.astype(jnp.int32)

    mine = turn_small(keep) - 1
    keep_forward = iota((lanes, cols), 1) % lane_dev == mine
    pair_of = iota((lane_dev, pairs), 1)
    owner = (pair_of // slots == iota((lane_dev, pairs), 0)).astype(BF16)
    tall = spread_out(partners_ref[...], owner)
    at_slot = iota((slots, pairs), 1) % slots == iota((slots, pairs), 0)
    target = jnp.sum(jnp.where(at_slot, tall, 0.0), axis=0, keepdims=True).astype(jnp.int32)
    pair_row = iota((1, pairs), 1)
    tall_column = turn_small(jnp.where(at_slot, tall, 0.0))
    pick = (tall_column == iota((pairs, lanes), 1)).astype(BF16)
    pick = jnp.concatenate([pick, pick], axis=1)
    keep_reverse = iota((pairs, cols), 1) % lane_dev == iota((pairs, cols), 0) // slots
    gather = (iota((FINE, cols), 1) // lane_dev == iota((FINE, cols), 0)).astype(BF16)
    place = (
        (target // lane_dev) * lane_dev + pair_row // slots == iota((lanes, pairs), 0)
    ).astype(BF16)
    counted = nn(
        jnp.broadcast_to(counts_ref[...], (8, lane_dev)).astype(F32).astype(BF16), owner
    )[0:1]
    gain = jnp.where((pair_row % slots).astype(F32) < counted, F32(scale), 0.0)

    def multiply(c):
        begin = c * wide
        width = wide + (HALF if c == chunks - 1 else 0)
        group = 2

        def body(step, carry):
            first = wall[:, begin : begin + width]
            second = wall[:, begin + HALF : begin + HALF + width]
            rows = jnp.concatenate([first, second], axis=0)
            for i in range(group):
                a = step * group + i
                start = pl.multiple_of(begin + HALF - FINE * a, FINE)
                term = nn(rows, refs[pl.ds(start, width), :])
                if c == 0:
                    acc[a] = term
                else:
                    acc[a] += term
            return carry

        lax.fori_loop(0, STEPS // group, body, 0)

    def relay(d, c):
        for side in range(2):
            way = 1 - 2 * side

            @pl.when(on_line(z - way * d))
            def _():
                block = block_of(z - way * d, True, c)
                remote(
                    block, block, send_d.at[d, side, c], recv_d.at[d, side, c],
                    {"lane": sibling},
                ).wait_recv()
                across(d, side, c).start()

            if d + 1 < n_z:
                @pl.when(on_line(z - way * d) & on_line(z + way))
                def _():
                    passed(d + 1, side, c).start()

    def complete(c):
        across(0, 0, c, False).wait_recv()
        for d in range(1, n_z):
            for side in range(2):
                @pl.when(on_line(z - (1 - 2 * side) * d))
                def _():
                    across(d, side, c, False).wait_recv()

    for slot in range(chunks + n_z - 1):
        for d in range(1, n_z):
            if 0 <= slot + 1 - d < chunks:
                relay(d, slot + 1 - d)
        c = slot + 1 - n_z
        if c == 0:
            take_w.wait()
        if c >= 0:
            complete(c)
            multiply(c)

    for off in list(range(1, n_rec)) + [0]:
        there = (rec + off) % n_rec
        count = lag_dev // FINE
        first = there * count
        rows = pl.ds(pl.multiple_of((first // STEPS) * lanes, lanes), lanes)
        blocks = [acc[first % STEPS + i, rows, :] for i in range(count)]
        kept = [jnp.where(keep_forward, block, 0.0) for block in blocks]
        split = [jnp.concatenate(pieces(block, 2), axis=0) for block in blocks]
        picked = nn(pick, jnp.concatenate(split, axis=1))
        for i in range(count):
            kept.append(jnp.where(keep_reverse, picked[:, i * cols : (i + 1) * cols], 0.0))
        kept = jnp.concatenate(kept, axis=0)
        summed = jnp.zeros((FINE, kept.shape[0]), F32)
        for part in pieces(kept, 2):
            summed += nt(gather, part)
        for i in range(count):
            at = slice(i * FINE, (i + 1) * FINE)
            zbuf[off, at, 0:lanes] = summed[:, i * lanes : (i + 1) * lanes]
            begin = count * lanes + i * pairs
            zbuf[off, at, lanes : lanes + pairs] = summed[:, begin : begin + pairs]
        if off > 0:
            go(remote(zbuf.at[off], zin.at[off], send_z.at[off], recv_z.at[off], {"rec": there}))

    total = zbuf[0]
    for off in range(1, n_rec):
        remote(
            zbuf.at[off], zin.at[off], send_z.at[off], recv_z.at[off], {"lane": sibling}
        ).wait_recv()
        total += zin[off]

    forward_sum = total[:, 0:lanes]
    if lag_dev < 128:
        forward_sum = jnp.concatenate(
            [forward_sum, jnp.zeros((128 - lag_dev, lanes), F32)], axis=0
        )
    fout[...] = forward_sum.T
    fin[rows_of(me), :] = fout[rows_of(me), :]
    for off in range(1, n_lane):
        there = (me + off) % n_lane
        go(
            remote(
                fout.at[rows_of(there), :], fin.at[rows_of(me), :],
                send_f.at[off], recv_f.at[off], {"lane": there},
            )
        )
    out_ref[1] = total[:, lanes : lanes + pairs] * gain
    for off in range(1, n_lane):
        block = fin.at[rows_of((me + n_lane - off) % n_lane), :]
        remote(block, block, send_f.at[off], recv_f.at[off], {"lane": sibling}).wait_recv()
    returned = fin[...].T[0:lag_dev]
    placed = nn(jnp.concatenate(pieces(returned, 3), axis=0), place)
    final = placed[0:lag_dev] + placed[lag_dev : 2 * lag_dev] + placed[2 * lag_dev :]
    out_ref[0] = final * gain
    for copy in sent:
        copy.wait_send()
    for c in range(chunks):
        own_across(c).wait_send()
        for side in range(2):
            way = 1 - 2 * side

            @pl.when(on_line(z + way))
            def _():
                passed(1, side, c, True).wait_send()

            for d in range(1, n_z):
                @pl.when(on_line(z - way * d))
                def _():
                    across(d, side, c).wait_send()

                if d + 1 < n_z:
                    @pl.when(on_line(z - way * d) & on_line(z + way))
                    def _():
                        passed(d + 1, side, c).wait_send()


def per_device(waveforms, patterns, partners, counts):
    lane_dev, time_dev = waveforms.shape
    slots = partners.shape[1]
    n_lane, n_rec = lax.axis_size("lane"), lax.axis_size("rec")
    lanes, pairs = lane_dev * n_lane, lane_dev * slots
    n_z = n_lane // 2
    lag_dev = LAGS // n_rec
    cols = FINE * lane_dev
    chunks = 4
    scale = (5.0 * time_dev * n_rec) ** -0.5
    dma = pltpu.SemaphoreType.DMA
    return pl.pallas_call(
        functools.partial(kernel, n_lane, n_rec, scale, chunks),
        out_shape=jax.ShapeDtypeStruct((2, lag_dev, pairs), F32),
        in_specs=[pl.BlockSpec(memory_space=pltpu.HBM)] * 2
        + [pl.BlockSpec(memory_space=pltpu.VMEM)] * 2,
        out_specs=pl.BlockSpec(memory_space=pltpu.VMEM),
        scratch_shapes=[
            pltpu.VMEM((lanes, time_dev + 2 * HALF), BF16),
            pltpu.VMEM((lane_dev, time_dev), jnp.int32),
            pltpu.VMEM((n_lane, slots, lanes), F32),
            pltpu.VMEM((lane_dev, LAGS), BF16),
            pltpu.VMEM((lane_dev, LAGS), BF16),
            pltpu.VMEM((cols, time_dev + LAGS), BF16),
            pltpu.VMEM((time_dev + LAGS, cols), BF16),
            pltpu.VMEM((STEPS, 2 * lanes, cols), F32),
            pltpu.VMEM((n_rec, lag_dev, lanes + pairs), F32),
            pltpu.VMEM((n_rec, lag_dev, lanes + pairs), F32),
            pltpu.VMEM((lanes, 128), F32),
            pltpu.VMEM((lanes, 128), F32),
            dma((1,)), dma((1,)),
            dma((n_z, 2, chunks)), dma((n_z, 2, chunks)),
            dma((n_z, 2, chunks)), dma((n_z, 2, chunks)),
            dma((n_lane,)), dma((n_lane,)),
            dma((1,)), dma((1,)),
            dma((n_rec,)), dma((n_rec,)),
            dma((n_lane,)), dma((n_lane,)),
        ],
        compiler_params=pltpu.CompilerParams(
            collective_id=0, has_side_effects=True, vmem_limit_bytes=(256 + lanes) * 64 * 1024
        ),
    )(waveforms, patterns, partners.T, counts[None, :])


def solution(mesh):
    in_specs = (P("lane", "rec"), P("lane", "rec"), P("lane", None), P("lane"))
    out_specs = P(None, "rec", "lane")
    return jax.shard_map(
        per_device, mesh=mesh, in_specs=in_specs, out_specs=out_specs, check_vma=False
    )
```
